256 devices in a mesh: group: 8 (over x, core), dev: 32 (over y, z).
Axes of the slice: x: 4, y: 4, z: 8, core: 2. Of those that a mesh axis runs over, the one named last changes fastest.
Arguments:
- embeddings: bfloat16 [262144, 1024], P(('group', 'dev')), may hold values from -200 to 200
- cluster_ids: int32 [262144], P(('group', 'dev')), may hold values from 0 to 255, never falling along the last dimension, each value on 1 to 2048 neighbouring positions
Outputs:
- earlier_peak: float32 [262144], P(('group', 'dev'))
- later_peak: float32 [262144], P(('group', 'dev'))
The draws below stay inside these ranges and needn't reach their ends.
Inputs may be any that keep to these rules, and one draw needn't show every extreme that they name: `cluster_ids`: cluster numbers never fall along the rows; each cluster holds 1 to 2048 rows, one exactly 2048.
All inputs are finite; a program needn't handle non-finite values.
Results may differ from the reference program's by a relative error of at most 0.00057.
Values may be sent and summed in bfloat16 or wider, within the bound.
No kernel may reach another device: no remote copies, remote signals or barrier semaphores. Data moves between devices by JAX's collectives and lax.ppermute only.
A program may use at most 64 MiB of HBM per device.

```python
import math
import jax
import jax.numpy as jnp
import numpy as np
from jax import lax

D = 1024
R_DEV = 1024
LOOK = 2
MOST = 2048
ROWS = 262144
CLUSTERS = 256


def draw_embeddings(key, part):
    key = jax.random.fold_in(key, 7)
    noise_key, weight_key, reach_key, scale_key = jax.random.split(key, 4)
    noise = jnp.clip(jax.random.normal(noise_key, (ROWS, D), jnp.float32), -4.0, 4.0)
    scales = jnp.exp(jax.random.uniform(scale_key, (ROWS,), jnp.float32, 0.0, math.log(10.0)))
    weights = jax.random.uniform(weight_key, (ROWS,), jnp.float32, 0.0, 2.0)
    distance = jax.random.randint(reach_key, (ROWS,), 1, MOST + 1)
    source = jnp.maximum(jnp.arange(ROWS, dtype=jnp.int32) - distance, 0)
    mixed = noise + weights[:, None] * noise[source]
    return (mixed * scales[:, None]).astype(jnp.bfloat16)


def length_profile(number_of, total, bound, slope):
    portions = [(1 << 20) // math.isqrt(rank ** slope) + 1 for rank in range(2, number_of + 1)]
    rest, counts = total - bound - (number_of - 1), [1] * (number_of - 1)
    while rest > 0:
        movable = [i for i in range(number_of - 1) if counts[i] < bound]
        pool, budget = sum([portions[i] for i in movable]), rest
        for i in movable:
            addition = min(bound - counts[i], max(1, budget * portions[i] // pool), rest)
            counts[i] = counts[i] + addition
            rest = rest - addition
    return np.array([bound] + counts)


def ragged_sizes(stream_key, number_of, total, bound, lean):
    if number_of == 2:
        one = jax.random.randint(stream_key, (), max(1, total - bound), min(bound, total - 1) + 1)
        return jnp.stack([one, total - one])
    lengths = jnp.asarray(length_profile(number_of, total, bound, lean), jnp.int32)
    twos = (number_of - 1) // 2
    source_of, sink = lengths[1:1 + 2 * twos:2], lengths[2:2 + 2 * twos:2]
    margin = jnp.minimum(source_of - 1, bound - sink)
    passed = jax.random.randint(jax.random.fold_in(stream_key, 1), (twos,), 0, 1 << 20) % (margin + 1)
    lengths = lengths.at[1:1 + 2 * twos:2].set(source_of - passed).at[2:2 + 2 * twos:2].set(sink + passed)
    return lengths[jax.random.permutation(jax.random.fold_in(stream_key, 2), number_of)]


def setup_inputs(seed: int = 0) -> dict:
    key_list = jax.random.split(jax.random.key(seed), 3)
    return {
        "embeddings": draw_embeddings(jax.random.fold_in(key_list[2], 71), 0),
        "cluster_ids": jnp.searchsorted(jnp.cumsum(ragged_sizes(key_list[1], CLUSTERS, ROWS, MOST, 2)), jnp.arange(ROWS), side="right").astype(jnp.int32),
    }


def unit_rows(values):
    wide = values.astype(jnp.float32)
    return (wide * lax.rsqrt(lax.optimization_barrier(jnp.sum(wide * wide, axis=1, keepdims=True)) + 1e-06)).astype(jnp.bfloat16)

def reference(embeddings, cluster_ids):
    normed = unit_rows(embeddings)
    block_count = ROWS // R_DEV
    lead_rows = LOOK * R_DEV
    padded_rows = jnp.concatenate([jnp.zeros((lead_rows, D), jnp.bfloat16), normed], axis=0)
    padded_ids = jnp.concatenate([jnp.full((lead_rows,), -1, jnp.int32), cluster_ids], axis=0)
    span = (LOOK + 1) * R_DEV

    def block_peaks(block_index):
        start = (block_index * R_DEV).astype(jnp.int32)
        tile_rows = lax.dynamic_slice_in_dim(normed, start, R_DEV, 0)
        row_labels = lax.dynamic_slice_in_dim(cluster_ids, start, R_DEV, 0)
        columns = lax.dynamic_slice_in_dim(padded_rows, start, span, 0)
        column_labels = lax.dynamic_slice_in_dim(padded_ids, start, span, 0)
        scores = lax.dot_general(tile_rows, columns, (((1,), (1,)), ((), ())), preferred_element_type=jnp.float32)
        row_place = jnp.arange(R_DEV, dtype=jnp.int32) + lead_rows
        column_place = jnp.arange(span, dtype=jnp.int32)
        allowed = (row_labels[:, None] == column_labels[None, :]) & (column_place[None, :] < row_place[:, None])
        masked = jnp.where(allowed, scores, jnp.float32(-1.0))
        return (lax.optimization_barrier(jnp.max(masked, axis=1)), lax.optimization_barrier(jnp.max(masked, axis=0)))
    row_peaks, column_maxima = lax.map(block_peaks, jnp.arange(block_count, dtype=jnp.int32))
    earlier_peak = row_peaks.reshape(ROWS)
    column_parts = column_maxima.reshape(block_count, LOOK + 1, R_DEV)
    column_parts = jnp.concatenate([column_parts, jnp.full((LOOK, LOOK + 1, R_DEV), -1.0, jnp.float32)], axis=0)
    later_blocks = jnp.full((block_count, R_DEV), -1.0, jnp.float32)
    for offset_step in range(LOOK + 1):
        later_blocks = jnp.maximum(later_blocks, column_parts[LOOK - offset_step:LOOK - offset_step + block_count, offset_step])
    return (earlier_peak, later_blocks.reshape(ROWS))
```

```python
import functools

import jax
import jax.numpy as jnp
from jax import lax
from jax.experimental import pallas as pl
from jax.experimental.pallas import tpu as pltpu
from jax.sharding import PartitionSpec as P

ROWS = 1024
WIDTH = 1024
TILE = 256
CHUNKS = (256, 512, 256)
VMEM_LIMIT = 40 * 1024 * 1024


def passed_along(block, distance):
    axes = ("group", "dev")
    devices = range(lax.axis_size(axes))
    route = [(i - distance, i) for i in devices if i - distance in devices]
    return lax.ppermute(block, axes, route)


def unit_rows(values):
    wide = values.astype(jnp.float32)
    return (wide * lax.rsqrt(jnp.sum(wide * wide, axis=1, keepdims=True) + 1e-06)).astype(
        jnp.bfloat16
    )


def products(rows, columns):
    return lax.dot_general(
        rows, columns, (((1,), (1,)), ((), ())), preferred_element_type=jnp.float32
    )


def tail_bound(before, after):
    last = before[:, ROWS - 1 :]
    count = jnp.sum((before == after[:, :1]).astype(jnp.int32), axis=1, keepdims=True)
    return jnp.where(after == last, ROWS - count, ROWS)


def head_bound(after, before):
    first = after[:, :1]
    count = jnp.sum((after == before[:, ROWS - 1 :]).astype(jnp.int32), axis=1, keepdims=True)
    return jnp.where(before == first, count, 0)


def peak_from(rows, start, columns_ref, bound_ref, peak_ref, is_earlier):
    count = rows.shape[0]
    place = lax.broadcasted_iota(jnp.int32, (count, TILE), 0) + start

    def step(tile, carry):
        at = pl.ds(pl.multiple_of(tile * TILE, TILE), TILE)
        scores = products(rows, columns_ref[at, :])
        bound = bound_ref[:, at]
        allowed = (place >= bound) if is_earlier else (place < bound)
        best = jnp.max(jnp.where(allowed, scores, -1.0), axis=0, keepdims=True)
        peak_ref[:, at] = jnp.maximum(peak_ref[:, at], best)
        return carry

    lax.fori_loop(0, columns_ref.shape[0] // TILE, step, 0)


def own_kernel(raw_ref, row_labels_ref, column_labels_ref, normed_ref, earlier_ref, later_ref):
    def norm_step(tile, carry):
        at = pl.ds(pl.multiple_of(tile * TILE, TILE), TILE)
        normed_ref[at, :] = unit_rows(raw_ref[at, :])
        return carry

    lax.fori_loop(0, ROWS // TILE, norm_step, 0)
    earlier_ref[...] = jnp.full_like(earlier_ref, -1.0)
    later_ref[...] = jnp.full_like(later_ref, -1.0)

    def step(index, carry):
        row_tile = index // (ROWS // TILE)
        tile = index % (ROWS // TILE)
        rows_at = pl.ds(pl.multiple_of(row_tile * TILE, TILE), TILE)
        at = pl.ds(pl.multiple_of(tile * TILE, TILE), TILE)
        scores = products(normed_ref[rows_at, :], normed_ref[at, :])
        shared = row_labels_ref[rows_at, :] == column_labels_ref[:, at]
        masked = jnp.where(shared, scores, -1.0)
        place = lax.broadcasted_iota(jnp.int32, (TILE, TILE), 0) + row_tile * TILE
        other = lax.broadcasted_iota(jnp.int32, (TILE, TILE), 1) + tile * TILE
        before = jnp.max(jnp.where(place < other, masked, -1.0), axis=0, keepdims=True)
        after = jnp.max(jnp.where(place > other, masked, -1.0), axis=0, keepdims=True)
        earlier_ref[:, at] = jnp.maximum(earlier_ref[:, at], before)
        later_ref[:, at] = jnp.maximum(later_ref[:, at], after)
        return carry

    lax.fori_loop(0, (ROWS // TILE) ** 2, step, 0)


def full(shape, dtype):
    return jax.ShapeDtypeStruct(shape, dtype)


def call(kernel, outs, args, macs):
    return pl.pallas_call(
        kernel,
        out_shape=outs,
        in_specs=[pl.BlockSpec(memory_space=pltpu.VMEM)] * len(args),
        out_specs=[pl.BlockSpec(memory_space=pltpu.VMEM)] * len(outs),
        compiler_params=pltpu.CompilerParams(vmem_limit_bytes=VMEM_LIMIT),
        cost_estimate=pl.CostEstimate(
            flops=2 * macs, bytes_accessed=8 * 1024 * 1024, transcendentals=ROWS
        ),
    )(*args)


VECTOR = full((1, ROWS), jnp.float32)


def bridge_kernel(step, *refs):
    prefix = [sum(CHUNKS[:k]) for k in range(len(CHUNKS) + 1)]
    size = CHUNKS[step]
    seen = step + 1
    raw_before, raw_after = refs[:2]
    olds_before = refs[2 : 2 + step]
    olds_after = refs[2 + step : 2 + 2 * step]
    labels_before, labels_after, was_later, was_earlier = refs[2 + 2 * step : 6 + 2 * step]
    new_before, new_after, later_before, earlier_after = refs[6 + 2 * step : 10 + 2 * step]
    bound_before, bound_after = refs[10 + 2 * step :]
    new_before[...] = unit_rows(raw_before[...])
    new_after[...] = unit_rows(raw_after[...])
    later_before[...] = was_later[...]
    earlier_after[...] = was_earlier[...]
    bound_before[...] = head_bound(labels_after[...], labels_before[...])
    bound_after[...] = tail_bound(labels_before[...], labels_after[...])
    befores = list(olds_before) + [new_before]
    afters = list(olds_after) + [new_after]
    for i in range(seen):
        for j in range(seen):
            if max(i, j) != step or prefix[i] + prefix[j] + 2 > ROWS:
                continue
            low_before = ROWS - prefix[i + 1]
            low_after = prefix[j]
            peak_from(
                befores[i][...],
                low_before,
                afters[j],
                bound_after.at[:, pl.ds(low_after, CHUNKS[j])],
                earlier_after.at[:, pl.ds(low_after, CHUNKS[j])],
                True,
            )
            peak_from(
                afters[j][...],
                low_after,
                befores[i],
                bound_before.at[:, pl.ds(low_before, CHUNKS[i])],
                later_before.at[:, pl.ds(low_before, CHUNKS[i])],
                False,
            )


def side_kernel(step, before, after, normed, l_before, labels, l_after, e_in, l_in, e, l, b_e, b_l):
    prefix = sum(CHUNKS[:step])
    e[...] = e_in[...]
    l[...] = l_in[...]
    b_e[...] = tail_bound(l_before[...], labels[...])
    b_l[...] = head_bound(l_after[...], labels[...])
    peak_from(before[...], ROWS - prefix - CHUNKS[step], normed, b_e, e, True)
    peak_from(after[...], prefix, normed, b_l, l, False)


def with_scratch(kernel, outs, args, macs):
    return pl.pallas_call(
        kernel,
        out_shape=outs,
        in_specs=[pl.BlockSpec(memory_space=pltpu.VMEM)] * len(args),
        out_specs=[pl.BlockSpec(memory_space=pltpu.VMEM)] * len(outs),
        scratch_shapes=[pltpu.VMEM((1, ROWS), jnp.int32)] * 2,
        compiler_params=pltpu.CompilerParams(vmem_limit_bytes=VMEM_LIMIT),
        cost_estimate=pl.CostEstimate(
            flops=2 * macs, bytes_accessed=8 * 1024 * 1024, transcendentals=ROWS
        ),
    )(*args)


def per_device(embeddings, cluster_ids):
    steps = len(CHUNKS)
    prefix = [sum(CHUNKS[:k]) for k in range(steps + 1)]
    before, after = [], []
    source = embeddings
    for step in range(steps):
        tail = source[ROWS - prefix[step + 1] : ROWS - prefix[step]]
        head = source[prefix[step] : prefix[step + 1]]
        if step == 0:
            tail, head, source = lax.optimization_barrier((tail, head, source))
        before.append(passed_along(tail, 1))
        after.append(passed_along(head, -1))
    labels = cluster_ids + 1
    labels_before = passed_along(labels, 1).reshape(1, ROWS)
    labels_after = passed_along(labels, -1).reshape(1, ROWS)
    row = labels.reshape(1, ROWS)
    normed, earlier, later = call(
        own_kernel,
        [full((ROWS, WIDTH), jnp.bfloat16), VECTOR, VECTOR],
        (embeddings, labels.reshape(ROWS, 1), row),
        ROWS * ROWS * WIDTH,
    )
    befores, afters = [], []
    later_before = jnp.full((1, ROWS), -1.0, jnp.float32)
    earlier_after = jnp.full((1, ROWS), -1.0, jnp.float32)
    for step in range(steps):
        chunk = full((CHUNKS[step], WIDTH), jnp.bfloat16)
        new_before, new_after, later_before, earlier_after = with_scratch(
            functools.partial(bridge_kernel, step),
            [chunk, chunk, VECTOR, VECTOR],
            (
                before[step],
                after[step],
                *befores,
                *afters,
                labels_before,
                labels_after,
                later_before,
                earlier_after,
            ),
            2 * CHUNKS[step] * (ROWS - prefix[step]) * WIDTH,
        )
        befores.append(new_before)
        afters.append(new_after)
        if step == steps - 1:
            from_after = passed_along(later_before, -1)
            from_before = passed_along(earlier_after, 1)
        earlier, later = with_scratch(
            functools.partial(side_kernel, step),
            [VECTOR, VECTOR],
            (new_before, new_after, normed, labels_before, row, labels_after, earlier, later),
            2 * CHUNKS[step] * ROWS * WIDTH,
        )
    first = lax.axis_index(("group", "dev")) == 0
    last = lax.axis_index(("group", "dev")) == lax.axis_size(("group", "dev")) - 1
    earlier = jnp.maximum(earlier, jnp.where(first, -1.0, from_before))
    later = jnp.maximum(later, jnp.where(last, -1.0, from_after))
    return (earlier.reshape(ROWS), later.reshape(ROWS))


def solution(mesh):
    placed = (P(("group", "dev"), None), P(("group", "dev")))
    return jax.shard_map(
        per_device,
        mesh=mesh,
        in_specs=placed,
        out_specs=(P(("group", "dev")), P(("group", "dev"))),
        check_vma=False,
    )
```

```python
import functools

import jax
import jax.numpy as jnp
from jax import lax
from jax.experimental import pallas as pl
from jax.experimental.pallas import tpu as pltpu
from jax.sharding import PartitionSpec as P

ROWS = 1024
WIDTH = 1024
TILE = 256
CHUNKS = ((0, 256), (768, 256), (256, 384), (640, 128))
NOTE = 16
RADIX = 32
VMEM_LIMIT = 16 * 1024 * 1024
AXES = ("group", "dev")


def exchanged(block, side):
    devices = lax.axis_size(AXES)
    pairs = [(i, i + 1) for i in range(side, devices - 1, 2)]
    return lax.ppermute(block, AXES, pairs + [(b, a) for a, b in pairs])


def both_sides(block):
    return [exchanged(block, side) for side in range(2)]


def by_role(side_0, side_1):
    odd = lax.axis_index("dev") % 2 == 1
    return jnp.where(odd, side_0, side_1), jnp.where(odd, side_1, side_0)


def unit_rows(values):
    wide = values.astype(jnp.float32)
    return (wide * lax.rsqrt(jnp.sum(wide * wide, axis=1, keepdims=True) + 1e-06)).astype(
        jnp.bfloat16
    )


def products(rows, columns):
    return lax.dot_general(
        rows, columns, (((1,), (1,)), ((), ())), preferred_element_type=jnp.float32
    )


def places(shape, axis):
    return lax.broadcasted_iota(jnp.int32, shape, axis)


def best_allowed(allowed, scores):
    return jnp.max(jnp.where(allowed, scores, -1.0), axis=0, keepdims=True)


def raise_peak(peaks_ref, row, at, best):
    row = slice(row, row + 1)
    peaks_ref[row, at] = jnp.maximum(peaks_ref[row, at], best)


def edge_run(ids, edge):
    label = ids[:, edge : edge + 1]
    return label, jnp.sum((ids == label).astype(jnp.int32), axis=1, keepdims=True)


def written_note(ids):
    row = places((NOTE, WIDTH), 0)
    note = jnp.zeros((NOTE, WIDTH), jnp.int32)
    for k, edge in enumerate((0, ROWS - 1)):
        label, count = edge_run(ids, edge)
        for n, value in enumerate((label, count // RADIX, count % RADIX)):
            note = jnp.where(row == 3 * k + n, value, note)
    return note.astype(jnp.float32).astype(jnp.bfloat16)


def read_note(note, k):
    note = note.astype(jnp.float32).astype(jnp.int32)
    label, high, low = (note[3 * k + n : 3 * k + n + 1, 0:1] for n in range(3))
    return label, high * RADIX + low


def noted_kernel(raw_hbm, _, ids_ref, piece_ref, sem):
    start, size = CHUNKS[1]
    copy = pltpu.make_async_copy(
        raw_hbm.at[pl.ds(start, size)], piece_ref.at[pl.ds(0, size)], sem
    )
    copy.start()
    piece_ref[size:, :] = written_note(ids_ref[...])
    copy.wait()


def own_kernel(
    _, __, raw_ref, row_ids_ref, ids_ref, normed_ref, earlier_ref, later_ref, piece_ref
):
    start, size = CHUNKS[2]
    piece_ref[...] = raw_ref[start : start + size, :]
    for part in range(0, ROWS, 128):
        normed_ref[part : part + 128, :] = unit_rows(raw_ref[part : part + 128, :])
    earlier_ref[...] = jnp.full_like(earlier_ref, -1.0)
    later_ref[...] = jnp.full_like(later_ref, -1.0)
    tiles = ROWS // TILE
    for row_tile in range(tiles):
        rows_at = pl.ds(row_tile * TILE, TILE)
        rows = normed_ref[rows_at, :]
        for tile in range(tiles):
            at = pl.ds(tile * TILE, TILE)
            scores = products(rows, normed_ref[at, :])
            shared = row_ids_ref[rows_at, :] == ids_ref[:, at]
            row, column = places(shared.shape, 0), places(shared.shape, 1)
            if row_tile <= tile:
                allowed = shared & (row < column) if row_tile == tile else shared
                raise_peak(earlier_ref, 0, at, best_allowed(allowed, scores))
            if row_tile >= tile:
                allowed = shared & (row > column) if row_tile == tile else shared
                raise_peak(later_ref, 0, at, best_allowed(allowed, scores))


OWN_BEFORE, OWN_AFTER, AFTER_BEFORE, BEFORE_AFTER, HAS_BEFORE, HAS_AFTER = range(6)


def find_bounds(ids, note_before, note_after, bounds):
    (label_before, count_before) = read_note(note_before, 1)
    (label_after, count_after) = read_note(note_after, 0)
    first_before = ROWS - count_before
    joined = label_before == label_after
    place = places((1, ROWS), 1)
    rows = {
        OWN_BEFORE: jnp.where(ids == label_before, first_before, ROWS),
        OWN_AFTER: jnp.where(ids == label_after, count_after, 0),
        AFTER_BEFORE: jnp.where(joined & (place < count_after), first_before, ROWS),
        BEFORE_AFTER: jnp.where(joined & (place >= first_before), count_after, 0),
        HAS_BEFORE: jnp.broadcast_to(count_before, (1, ROWS)),
        HAS_AFTER: jnp.broadcast_to(count_after, (1, ROWS)),
    }
    for row, value in rows.items():
        bounds[row : row + 1, :] = value


def against_own(chunk, before, after, normed_ref, bounds, peaks):
    start, size = CHUNKS[chunk]
    place = places((size, TILE), 0) + start
    rows = jnp.concatenate([before[...], after[...]], axis=0) if size < TILE else None
    for tile in range(ROWS // TILE):
        at = pl.ds(tile * TILE, TILE)
        columns = normed_ref[at, :]
        if rows is None:
            scores = products(before[...], columns), products(after[...], columns)
        else:
            scores = products(rows, columns)
            scores = scores[:size], scores[size:]
        allowed = place >= bounds[OWN_BEFORE : OWN_BEFORE + 1, at]
        raise_peak(peaks, 0, at, best_allowed(allowed, scores[0]))
        allowed = place < bounds[OWN_AFTER : OWN_AFTER + 1, at]
        raise_peak(peaks, 1, at, best_allowed(allowed, scores[1]))


def across(chunk, befores, afters, bounds, returned):
    for i in range(chunk + 1):
        for j in range(chunk + 1):
            (low_i, size_i), (low_j, size_j) = CHUNKS[i], CHUNKS[j]
            skip_i = max(0, low_j - low_i)
            size_j = min(size_j, low_i + size_i - low_j)
            if max(i, j) != chunk or skip_i >= size_i or size_j <= 0:
                continue
            low_i, size_i = low_i + skip_i, size_i - skip_i
            rows_i = befores[i].at[pl.ds(skip_i, size_i)]
            rows_j = afters[j].at[pl.ds(0, size_j)]
            for part in range(0, size_j, TILE):
                size = min(TILE, size_j - part)
                at = pl.ds(low_j + part, size)
                scores = products(rows_i[...], rows_j[part : part + size, :])
                bound = bounds[AFTER_BEFORE : AFTER_BEFORE + 1, at]
                allowed = places(scores.shape, 0) + low_i >= bound
                raise_peak(returned, 1, at, best_allowed(allowed, scores))
            for part in range(0, size_i, TILE):
                size = min(TILE, size_i - part)
                at = pl.ds(low_i + part, size)
                scores = products(rows_j[...], rows_i[part : part + size, :])
                bound = bounds[BEFORE_AFTER : BEFORE_AFTER + 1, at]
                allowed = places(scores.shape, 0) + low_j < bound
                raise_peak(returned, 0, at, best_allowed(allowed, scores))


def take_chunk(side_0, side_1, before, after):
    for part in range(0, before.shape[0], 128):
        at = slice(part, part + 128)
        before[at, :], after[at, :] = by_role(unit_rows(side_0[at, :]), unit_rows(side_1[at, :]))


def first_kernel(raw_ref, *refs):
    got, (normed, ids_ref, _) = (refs[0:2], refs[2:4]), refs[4:7]
    befores, afters = refs[7:9], refs[9:11]
    bounds, peaks, returned, piece_ref = refs[11:]
    start, size = CHUNKS[3]
    piece_ref[...] = raw_ref[start : start + size, :]
    peaks[...] = jnp.full_like(peaks, -1.0)
    returned[...] = jnp.full_like(returned, -1.0)
    notes = by_role(*(side[CHUNKS[1][1] :, :128].astype(jnp.float32) for side in got[1]))
    find_bounds(ids_ref[...], *notes, bounds)
    for chunk in range(2):
        take_chunk(*got[chunk], befores[chunk], afters[chunk])
        against_own(chunk, befores[chunk], afters[chunk], normed, bounds, peaks)
        across(chunk, befores, afters, bounds, returned)


def next_kernel(chunk, side_0, side_1, normed, bounds, peaks_in, returned_in, *refs):
    befores, afters = refs[:chunk], refs[chunk : 2 * chunk]
    before, after, peaks, returned = refs[2 * chunk :]
    peaks[...] = peaks_in[...]
    returned[...] = returned_in[...]
    take_chunk(side_0, side_1, before, after)
    against_own(chunk, before, after, normed, bounds, peaks)
    across(chunk, [*befores, before], [*afters, after], bounds, returned)


def last_across_kernel(chunk, side_0, side_1, bounds, returned_in, *refs):
    befores, afters = refs[:chunk], refs[chunk : 2 * chunk]
    before, after, returned = refs[2 * chunk :]
    returned[...] = returned_in[...]
    take_chunk(side_0, side_1, before, after)
    across(chunk, [*befores, before], [*afters, after], bounds, returned)


def last_own_kernel(chunk, before, after, normed, bounds, peaks_in, peaks):
    peaks[...] = peaks_in[...]
    against_own(chunk, before, after, normed, bounds, peaks)


def join_kernel(earlier_in, later_in, peaks, bounds, side_0, side_1, earlier, later):
    from_before, from_after = by_role(side_0[...], side_1[...])
    has_before = bounds[HAS_BEFORE : HAS_BEFORE + 1, :] > 0
    has_after = bounds[HAS_AFTER : HAS_AFTER + 1, :] > 0
    from_before = jnp.where(has_before, from_before[1:2], -1.0)
    from_after = jnp.where(has_after, from_after[0:1], -1.0)
    earlier[...] = jnp.maximum(jnp.maximum(earlier_in[...], peaks[0:1, :]), from_before)
    later[...] = jnp.maximum(jnp.maximum(later_in[...], peaks[1:2, :]), from_after)


def call(kernel, outs, args, in_hbm=0, scratch=()):
    in_vmem = pl.BlockSpec(memory_space=pltpu.VMEM)
    return pl.pallas_call(
        kernel,
        out_shape=outs,
        in_specs=[pl.BlockSpec(memory_space=pl.ANY)] * in_hbm + [in_vmem] * (len(args) - in_hbm),
        out_specs=[in_vmem] * len(outs),
        scratch_shapes=scratch,
        compiler_params=pltpu.CompilerParams(vmem_limit_bytes=VMEM_LIMIT),
        cost_estimate=pl.CostEstimate(flops=1024, bytes_accessed=1024, transcendentals=0),
    )(*args)


def vectors(count, dtype=jnp.float32):
    return jax.ShapeDtypeStruct((count, ROWS), dtype)


def piece(rows):
    return jax.ShapeDtypeStruct((rows, WIDTH), jnp.bfloat16)


def per_device(embeddings, cluster_ids):
    ids = cluster_ids.reshape(1, ROWS)
    start, size = CHUNKS[0]
    cut = embeddings[start : start + size]
    got = [both_sides(cut)]
    (cut,) = call(
        noted_kernel,
        [piece(CHUNKS[1][1] + NOTE)],
        (embeddings, cut, ids),
        in_hbm=2,
        scratch=[pltpu.SemaphoreType.DMA],
    )
    got.append(both_sides(cut))
    normed, earlier, later, cut = call(
        own_kernel,
        [piece(ROWS), vectors(1), vectors(1), piece(CHUNKS[2][1])],
        (*got[0], embeddings, cluster_ids.reshape(ROWS, 1), ids),
        in_hbm=2,
    )
    got.append(both_sides(cut))
    sizes = [piece(size) for _, size in CHUNKS]
    *new, bounds, peaks, returned, cut = call(
        first_kernel,
        [*sizes[:2], *sizes[:2], vectors(8, jnp.int32), vectors(2), vectors(2), sizes[3]],
        (embeddings, *got[0], *got[1], normed, ids, earlier),
    )
    got.append(both_sides(cut))
    befores, afters = new[:2], new[2:]
    before, after, peaks, returned = call(
        functools.partial(next_kernel, 2),
        [sizes[2], sizes[2], vectors(2), vectors(2)],
        (*got[2], normed, bounds, peaks, returned, *befores, *afters),
    )
    befores.append(before)
    afters.append(after)
    before, after, returned = call(
        functools.partial(last_across_kernel, 3),
        [sizes[3], sizes[3], vectors(2)],
        (*got[3], bounds, returned, *befores, *afters),
    )
    sent_back = both_sides(returned)
    (peaks,) = call(
        functools.partial(last_own_kernel, 3),
        [vectors(2)],
        (before, after, normed, bounds, peaks),
    )
    earlier, later = call(
        join_kernel, [vectors(1), vectors(1)], (earlier, later, peaks, bounds, *sent_back)
    )
    return (earlier.reshape(ROWS), later.reshape(ROWS))


def solution(mesh):
    placed = (P(AXES, None), P(AXES))
    return jax.shard_map(
        per_device,
        mesh=mesh,
        in_specs=placed,
        out_specs=(P(AXES), P(AXES)),
        check_vma=False,
    )
```

```python
import functools

import jax
import jax.numpy as jnp
from jax import lax
from jax.experimental import pallas as pl
from jax.experimental.pallas import tpu as pltpu
from jax.sharding import PartitionSpec as P

ROWS = 1024
WIDTH = 1024
TILE = 256
EDGE = 128
TO_AFTER = ((256, 256), (128, 128), (ROWS - EDGE, EDGE), (512, 384), (0, EDGE))
TO_BEFORE = ((256, 256), (128, 128), (0, EDGE), (512, 384), (ROWS - EDGE, EDGE))
SIZES = tuple(size for _, size in TO_AFTER)
NOTE = 16
RADIX = 32
VMEM_LIMIT = 16 * 1024 * 1024
AXES = ("group", "dev")


def exchanged(*blocks):
    devices = lax.axis_size(AXES)
    got = []
    for side, block in enumerate(blocks):
        pairs = [(i, i + 1) for i in range(side, devices - 1, 2)]
        got.append(lax.ppermute(block, AXES, pairs + [(b, a) for a, b in pairs]))
    return got


def faces_after(side):
    return lax.axis_index("dev") % 2 == side


def by_role(side_0, side_1):
    odd = lax.axis_index("dev") % 2 == 1
    return jnp.where(odd, side_0, side_1), jnp.where(odd, side_1, side_0)


def unit_rows(values):
    wide = values.astype(jnp.float32)
    return (wide * lax.rsqrt(jnp.sum(wide * wide, axis=1, keepdims=True) + 1e-06)).astype(
        jnp.bfloat16
    )


def products(rows, columns):
    return lax.dot_general(
        rows, columns, (((1,), (1,)), ((), ())), preferred_element_type=jnp.float32
    )


def places(shape, axis):
    return lax.broadcasted_iota(jnp.int32, shape, axis)


def best_allowed(allowed, scores):
    return jnp.max(jnp.where(allowed, scores, -1.0), axis=0, keepdims=True)


def raise_peak(peaks_ref, row, at, best):
    row = slice(row, row + 1)
    peaks_ref[row, at] = jnp.maximum(peaks_ref[row, at], best)


def edge_run(ids, edge):
    label = ids[:, edge : edge + 1]
    return label, jnp.sum((ids == label).astype(jnp.int32), axis=1, keepdims=True)


def written_note(ids):
    row = places((NOTE, WIDTH), 0)
    note = jnp.zeros((NOTE, WIDTH), jnp.int32)
    for k, edge in enumerate((0, ROWS - 1)):
        label, count = edge_run(ids, edge)
        for n, value in enumerate((label, count // RADIX, count % RADIX)):
            note = jnp.where(row == 3 * k + n, value, note)
    return note.astype(jnp.float32).astype(jnp.bfloat16)


def read_note(note, k):
    note = note.astype(jnp.float32).astype(jnp.int32)
    label, high, low = (note[3 * k + n : 3 * k + n + 1, 0:1] for n in range(3))
    return label, high * RADIX + low


def cut_copy(raw_hbm, chunk, side, piece_ref, sem):
    (low, size), (other_low, _) = TO_AFTER[chunk], TO_BEFORE[chunk]
    if low != other_low:
        low = pl.multiple_of(jnp.where(faces_after(side), low, other_low), EDGE)
    copy = pltpu.make_async_copy(raw_hbm.at[pl.ds(low, size)], piece_ref, sem)
    copy.start()
    return copy


def noted_kernel(raw_hbm, _, ids_ref, *refs):
    pieces, sems = refs[:2], refs[2]
    copies = []
    for side in range(2):
        for k, chunk in enumerate((1, 2)):
            rows = pieces[side].at[pl.ds(k * EDGE, EDGE)]
            copies.append(cut_copy(raw_hbm, chunk, side, rows, sems.at[2 * side + k]))
    note = written_note(ids_ref[...])
    for piece_ref in pieces:
        piece_ref[2 * EDGE :, :] = note
    for copy in copies:
        copy.wait()


def middle_kernel(raw_hbm, _, __, piece_ref, sem):
    cut_copy(raw_hbm, 3, 0, piece_ref, sem).wait()


def own_kernel(raw_ref, row_ids_ref, ids_ref, normed_ref, earlier_ref, later_ref):
    for part in range(0, ROWS, 128):
        normed_ref[part : part + 128, :] = unit_rows(raw_ref[part : part + 128, :])
    earlier_ref[...] = jnp.full_like(earlier_ref, -1.0)
    later_ref[...] = jnp.full_like(later_ref, -1.0)
    tiles = ROWS // TILE
    for row_tile in range(tiles):
        rows_at = pl.ds(row_tile * TILE, TILE)
        rows = normed_ref[rows_at, :]
        for tile in range(tiles):
            at = pl.ds(tile * TILE, TILE)
            scores = products(rows, normed_ref[at, :])
            shared = row_ids_ref[rows_at, :] == ids_ref[:, at]
            row, column = places(shared.shape, 0), places(shared.shape, 1)
            if row_tile <= tile:
                allowed = shared & (row < column) if row_tile == tile else shared
                raise_peak(earlier_ref, 0, at, best_allowed(allowed, scores))
            if row_tile >= tile:
                allowed = shared & (row > column) if row_tile == tile else shared
                raise_peak(later_ref, 0, at, best_allowed(allowed, scores))


OWN_BEFORE, OWN_AFTER, AFTER_BEFORE = range(3)
COUNT_BEFORE, COUNT_AFTER, OWN_HEAD, OWN_TAIL = range(4, 8)


def find_bounds(ids, note_before, note_after, bounds):
    (label_before, count_before) = read_note(note_before, 1)
    (label_after, count_after) = read_note(note_after, 0)
    first_before = ROWS - count_before
    joined = label_before == label_after
    place = places((1, ROWS), 1)
    rows = {
        OWN_BEFORE: jnp.where(ids == label_before, first_before, ROWS),
        OWN_AFTER: jnp.where(ids == label_after, count_after, 0),
        AFTER_BEFORE: jnp.where(joined & (place < count_after), first_before, ROWS),
    }
    own_head = jnp.sum((ids == label_before).astype(jnp.int32), axis=1, keepdims=True)
    own_tail = jnp.sum((ids == label_after).astype(jnp.int32), axis=1, keepdims=True)
    counts = (COUNT_BEFORE, count_before), (COUNT_AFTER, count_after)
    for row, count in (*counts, (OWN_HEAD, own_head), (OWN_TAIL, own_tail)):
        rows[row] = jnp.broadcast_to(count, (1, ROWS))
    for row, value in rows.items():
        bounds[row : row + 1, :] = value


def read_counts(bounds):
    return [jnp.max(bounds[row : row + 1, :128]) for row in range(4, 8)]


def against_own(chunk, before, after, normed_ref, bounds, peaks):
    size = SIZES[chunk]
    low_before, low_after = TO_AFTER[chunk][0], TO_BEFORE[chunk][0]
    tiles = [pl.ds(tile * TILE, TILE) for tile in range(ROWS // TILE)]

    def raise_own(row, at, scores):
        place = places(scores.shape, 0) + (low_after if row else low_before)
        bound = bounds[OWN_BEFORE + row : OWN_BEFORE + row + 1, at]
        allowed = (place < bound) if row else (place >= bound)
        raise_peak(peaks, row, at, best_allowed(allowed, scores))

    if size < TILE:
        rows = jnp.concatenate([before[...], after[...]], axis=0)
        for at in tiles:
            scores = products(rows, normed_ref[at, :])
            raise_own(0, at, scores[:size])
            raise_own(1, at, scores[size:])
        return
    count_before, count_after, own_head, own_tail = read_counts(bounds)

    @pl.when((ROWS - count_before < low_before + size) & (own_head > 0))
    def _():
        for at in tiles:
            raise_own(0, at, products(before[...], normed_ref[at, :]))

    @pl.when((count_after > low_after) & (own_tail > 0))
    def _():
        for at in tiles:
            raise_own(1, at, products(after[...], normed_ref[at, :]))


def across(chunk, befores, afters, bounds, returned):
    _, _, own_head, own_tail = read_counts(bounds)

    @pl.when((own_head == ROWS) & (own_tail == ROWS))
    def _():
        for i in range(chunk + 1):
            for j in range(chunk + 1):
                if max(i, j) == chunk:
                    across_pieces(befores[i], *TO_AFTER[i], afters[j], *TO_BEFORE[j], bounds, returned)


def across_pieces(before, low_i, size_i, after, low_j, size_j, bounds, returned):
    skip_i = max(0, low_j - low_i)
    size_j = min(size_j, low_i + size_i - low_j)
    if skip_i >= size_i or size_j <= 0:
        return
    low_i, size_i = low_i + skip_i, size_i - skip_i
    rows = before[skip_i : skip_i + size_i, :]
    best = jnp.full((size_i, 128), -1.0, jnp.float32)
    for part in range(0, size_j, TILE):
        size = min(TILE, size_j - part)
        at = pl.ds(low_j + part, size)
        scores = products(rows, after[part : part + size, :])
        bound = bounds[AFTER_BEFORE : AFTER_BEFORE + 1, at]
        masked = jnp.where(places(scores.shape, 0) + low_i >= bound, scores, -1.0)
        raise_peak(returned, 1, at, jnp.max(masked, axis=0, keepdims=True))
        for lanes in range(0, size, 128):
            best = jnp.maximum(best, masked[:, lanes : lanes + 128])
    raise_peak(returned, 0, pl.ds(low_i, size_i), jnp.max(best.T, axis=0, keepdims=True))


def take_chunk(side_0, side_1, before, after):
    for part in range(0, before.shape[0], 128):
        at = slice(part, part + 128)
        before[at, :], after[at, :] = by_role(unit_rows(side_0[at, :]), unit_rows(side_1[at, :]))


def first_kernel(raw_hbm, *refs):
    (first, noted), (normed, ids_ref, _) = (refs[0:2], refs[2:4]), refs[4:7]
    befores, afters = refs[7:10], refs[10:13]
    bounds, peaks, returned = refs[13:16]
    pieces, sems = refs[16:18], refs[18]
    copies = [cut_copy(raw_hbm, 4, side, pieces[side], sems.at[side]) for side in range(2)]
    peaks[...] = jnp.full_like(peaks, -1.0)
    returned[...] = jnp.full_like(returned, -1.0)
    notes = by_role(*(side[2 * EDGE :, :128].astype(jnp.float32) for side in noted))
    find_bounds(ids_ref[...], *notes, bounds)
    got = first, [side.at[pl.ds(0, EDGE)] for side in noted], [side.at[pl.ds(EDGE, EDGE)] for side in noted]
    for chunk in range(3):
        take_chunk(*got[chunk], befores[chunk], afters[chunk])
        against_own(chunk, befores[chunk], afters[chunk], normed, bounds, peaks)
        across(chunk, befores, afters, bounds, returned)
    for copy in copies:
        copy.wait()


def next_kernel(chunk, side_0, side_1, normed, bounds, peaks_in, returned_in, *refs):
    befores, afters = refs[:chunk], refs[chunk : 2 * chunk]
    before, after, peaks, returned = refs[2 * chunk :]
    peaks[...] = peaks_in[...]
    returned[...] = returned_in[...]
    take_chunk(side_0, side_1, before, after)
    against_own(chunk, before, after, normed, bounds, peaks)
    across(chunk, [*befores, before], [*afters, after], bounds, returned)


def last_across_kernel(chunk, side_0, side_1, bounds, returned_in, *refs):
    befores, afters = refs[:chunk], refs[chunk : 2 * chunk]
    before, after, returned = refs[2 * chunk :]
    returned[...] = returned_in[...]
    take_chunk(side_0, side_1, before, after)
    across(chunk, [*befores, before], [*afters, after], bounds, returned)


def last_own_kernel(chunk, before, after, normed, bounds, peaks_in, peaks):
    peaks[...] = peaks_in[...]
    against_own(chunk, before, after, normed, bounds, peaks)


def join_kernel(earlier_in, later_in, peaks, bounds, side_0, side_1, earlier, later):
    from_before, from_after = by_role(side_0[...], side_1[...])
    has_before = bounds[COUNT_BEFORE : COUNT_BEFORE + 1, :] > 0
    has_after = bounds[COUNT_AFTER : COUNT_AFTER + 1, :] > 0
    from_before = jnp.where(has_before, from_before[1:2], -1.0)
    from_after = jnp.where(has_after, from_after[0:1], -1.0)
    earlier[...] = jnp.maximum(jnp.maximum(earlier_in[...], peaks[0:1, :]), from_before)
    later[...] = jnp.maximum(jnp.maximum(later_in[...], peaks[1:2, :]), from_after)


def call(kernel, outs, args, in_hbm=0, scratch=()):
    in_vmem = pl.BlockSpec(memory_space=pltpu.VMEM)
    return pl.pallas_call(
        kernel,
        out_shape=outs,
        in_specs=[pl.BlockSpec(memory_space=pl.ANY)] * in_hbm + [in_vmem] * (len(args) - in_hbm),
        out_specs=[in_vmem] * len(outs),
        scratch_shapes=scratch,
        compiler_params=pltpu.CompilerParams(vmem_limit_bytes=VMEM_LIMIT),
        cost_estimate=pl.CostEstimate(flops=1024, bytes_accessed=1024, transcendentals=0),
    )(*args)


def vectors(count, dtype=jnp.float32):
    return jax.ShapeDtypeStruct((count, ROWS), dtype)


def piece(rows):
    return jax.ShapeDtypeStruct((rows, WIDTH), jnp.bfloat16)


def per_device(embeddings, cluster_ids):
    ids = cluster_ids.reshape(1, ROWS)
    low, size = TO_AFTER[0]
    cut = embeddings[low : low + size]
    first = exchanged(cut, cut)
    cuts = call(
        noted_kernel,
        [piece(2 * EDGE + NOTE)] * 2,
        (embeddings, cut, ids),
        in_hbm=2,
        scratch=[pltpu.SemaphoreType.DMA((4,))],
    )
    noted = exchanged(*cuts)
    (cut,) = call(
        middle_kernel,
        [piece(SIZES[3])],
        (embeddings, *first),
        in_hbm=3,
        scratch=[pltpu.SemaphoreType.DMA],
    )
    middle = exchanged(cut, cut)
    normed, earlier, later = call(
        own_kernel,
        [piece(ROWS), vectors(1), vectors(1)],
        (embeddings, cluster_ids.reshape(ROWS, 1), ids),
    )
    sizes = [piece(size) for size in SIZES]
    *new, bounds, peaks, returned, cut_0, cut_1 = call(
        first_kernel,
        [*sizes[:3], *sizes[:3], vectors(8, jnp.int32), vectors(2), vectors(2), sizes[4], sizes[4]],
        (embeddings, *first, *noted, normed, ids, earlier),
        in_hbm=1,
        scratch=[pltpu.SemaphoreType.DMA((2,))],
    )
    last = exchanged(cut_0, cut_1)
    befores, afters = new[:3], new[3:]
    before, after, peaks, returned = call(
        functools.partial(next_kernel, 3),
        [sizes[3], sizes[3], vectors(2), vectors(2)],
        (*middle, normed, bounds, peaks, returned, *befores, *afters),
    )
    befores.append(before)
    afters.append(after)
    before, after, returned = call(
        functools.partial(last_across_kernel, 4),
        [sizes[4], sizes[4], vectors(2)],
        (*last, bounds, returned, *befores, *afters),
    )
    sent_back = exchanged(returned, returned)
    (peaks,) = call(
        functools.partial(last_own_kernel, 4),
        [vectors(2)],
        (before, after, normed, bounds, peaks),
    )
    earlier, later = call(
        join_kernel, [vectors(1), vectors(1)], (earlier, later, peaks, bounds, *sent_back)
    )
    return (earlier.reshape(ROWS), later.reshape(ROWS))


def solution(mesh):
    placed = (P(AXES, None), P(AXES))
    return jax.shard_map(
        per_device,
        mesh=mesh,
        in_specs=placed,
        out_specs=(P(AXES), P(AXES)),
        check_vma=False,
    )
```

```python
import functools

import jax
import jax.numpy as jnp
from jax import lax
from jax.experimental import pallas as pl
from jax.experimental.pallas import tpu as pltpu
from jax.sharding import PartitionSpec as P

ROWS = 1024
WIDTH = 1024
TILE = 256
EDGE = 128
TO_AFTER = ((256, 256), (128, 128), (ROWS - EDGE, EDGE), (512, 384), (0, EDGE))
TO_BEFORE = ((256, 256), (128, 128), (0, EDGE), (512, 384), (ROWS - EDGE, EDGE))
SIZES = tuple(size for _, size in TO_AFTER)
NOTE = 16
RADIX = 32
VMEM_LIMIT = 16 * 1024 * 1024
AXES = ("group", "dev")


def exchanged(*blocks):
    devices = lax.axis_size(AXES)
    got = []
    for side, block in enumerate(blocks):
        pairs = [(i, i + 1) for i in range(side, devices - 1, 2)]
        got.append(lax.ppermute(block, AXES, pairs + [(b, a) for a, b in pairs]))
    return got


def faces_after(side):
    return lax.axis_index("dev") % 2 == side


def by_role(side_0, side_1):
    odd = lax.axis_index("dev") % 2 == 1
    return jnp.where(odd, side_0, side_1), jnp.where(odd, side_1, side_0)


def unit_rows(values):
    wide = values.astype(jnp.float32)
    return (wide * lax.rsqrt(jnp.sum(wide * wide, axis=1, keepdims=True) + 1e-06)).astype(
        jnp.bfloat16
    )


def products(rows, columns):
    return lax.dot_general(
        rows, columns, (((1,), (1,)), ((), ())), preferred_element_type=jnp.float32
    )


def places(shape, axis):
    return lax.broadcasted_iota(jnp.int32, shape, axis)


def best_allowed(allowed, scores):
    return jnp.max(jnp.where(allowed, scores, -1.0), axis=0, keepdims=True)


def raise_peak(peaks_ref, row, at, best):
    row = slice(row, row + 1)
    peaks_ref[row, at] = jnp.maximum(peaks_ref[row, at], best)


def edge_run(ids, edge):
    label = ids[:, edge : edge + 1]
    return label, jnp.sum((ids == label).astype(jnp.int32), axis=1, keepdims=True)


def written_note(ids):
    row = places((NOTE, WIDTH), 0)
    note = jnp.zeros((NOTE, WIDTH), jnp.int32)
    for k, edge in enumerate((0, ROWS - 1)):
        label, count = edge_run(ids, edge)
        for n, value in enumerate((label, count // RADIX, count % RADIX)):
            note = jnp.where(row == 3 * k + n, value, note)
    return note.astype(jnp.float32).astype(jnp.bfloat16)


def read_note(note, k):
    note = note.astype(jnp.float32).astype(jnp.int32)
    label, high, low = (note[3 * k + n : 3 * k + n + 1, 0:1] for n in range(3))
    return label, high * RADIX + low


def cut_copy(raw_hbm, chunk, side, piece_ref, sem):
    (low, size), (other_low, _) = TO_AFTER[chunk], TO_BEFORE[chunk]
    if low != other_low:
        low = pl.multiple_of(jnp.where(faces_after(side), low, other_low), EDGE)
    copy = pltpu.make_async_copy(raw_hbm.at[pl.ds(low, size)], piece_ref, sem)
    copy.start()
    return copy


def noted_kernel(raw_hbm, _, ids_ref, *refs):
    pieces, sems = refs[:2], refs[2]
    copies = []
    for side in range(2):
        for k, chunk in enumerate((1, 2)):
            rows = pieces[side].at[pl.ds(k * EDGE, EDGE)]
            copies.append(cut_copy(raw_hbm, chunk, side, rows, sems.at[2 * side + k]))
    note = written_note(ids_ref[...])
    for piece_ref in pieces:
        piece_ref[2 * EDGE :, :] = note
    for copy in copies:
        copy.wait()


def middle_kernel(raw_hbm, _, __, piece_ref, sem):
    cut_copy(raw_hbm, 3, 0, piece_ref, sem).wait()


def own_kernel(raw_ref, row_ids_ref, ids_ref, normed_ref, earlier_ref, later_ref):
    for part in range(0, ROWS, 128):
        normed_ref[part : part + 128, :] = unit_rows(raw_ref[part : part + 128, :])
    earlier_ref[...] = jnp.full_like(earlier_ref, -1.0)
    later_ref[...] = jnp.full_like(later_ref, -1.0)
    tiles = ROWS // TILE
    for row_tile in range(tiles):
        rows_at = pl.ds(row_tile * TILE, TILE)
        rows = normed_ref[rows_at, :]
        for tile in range(tiles):
            at = pl.ds(tile * TILE, TILE)
            scores = products(rows, normed_ref[at, :])
            shared = row_ids_ref[rows_at, :] == ids_ref[:, at]
            row, column = places(shared.shape, 0), places(shared.shape, 1)
            if row_tile <= tile:
                allowed = shared & (row < column) if row_tile == tile else shared
                raise_peak(earlier_ref, 0, at, best_allowed(allowed, scores))
            if row_tile >= tile:
                allowed = shared & (row > column) if row_tile == tile else shared
                raise_peak(later_ref, 0, at, best_allowed(allowed, scores))


OWN_BEFORE, OWN_AFTER, AFTER_BEFORE = range(3)
COUNT_BEFORE, COUNT_AFTER, OWN_HEAD, OWN_TAIL = range(4, 8)


def find_bounds(ids, note_before, note_after, bounds):
    (label_before, count_before) = read_note(note_before, 1)
    (label_after, count_after) = read_note(note_after, 0)
    first_before = ROWS - count_before
    joined = label_before == label_after
    place = places((1, ROWS), 1)
    rows = {
        OWN_BEFORE: jnp.where(ids == label_before, first_before, ROWS),
        OWN_AFTER: jnp.where(ids == label_after, count_after, 0),
        AFTER_BEFORE: jnp.where(joined & (place < count_after), first_before, ROWS),
    }
    own_head = jnp.sum((ids == label_before).astype(jnp.int32), axis=1, keepdims=True)
    own_tail = jnp.sum((ids == label_after).astype(jnp.int32), axis=1, keepdims=True)
    counts = (COUNT_BEFORE, count_before), (COUNT_AFTER, count_after)
    for row, count in (*counts, (OWN_HEAD, own_head), (OWN_TAIL, own_tail)):
        rows[row] = jnp.broadcast_to(count, (1, ROWS))
    for row, value in rows.items():
        bounds[row : row + 1, :] = value


def read_counts(bounds):
    return [jnp.max(bounds[row : row + 1, :128]) for row in range(4, 8)]


def against_own(chunk, before, after, normed_ref, bounds, peaks):
    size = SIZES[chunk]
    low_before, low_after = TO_AFTER[chunk][0], TO_BEFORE[chunk][0]
    tiles = [pl.ds(tile * TILE, TILE) for tile in range(ROWS // TILE)]

    def raise_own(row, at, scores):
        place = places(scores.shape, 0) + (low_after if row else low_before)
        bound = bounds[OWN_BEFORE + row : OWN_BEFORE + row + 1, at]
        allowed = (place < bound) if row else (place >= bound)
        raise_peak(peaks, row, at, best_allowed(allowed, scores))

    if size < TILE:
        rows = jnp.concatenate([before[...], after[...]], axis=0)
        for at in tiles:
            scores = products(rows, normed_ref[at, :])
            raise_own(0, at, scores[:size])
            raise_own(1, at, scores[size:])
        return
    count_before, count_after, own_head, own_tail = read_counts(bounds)

    @pl.when((ROWS - count_before < low_before + size) & (own_head > 0))
    def _():
        for at in tiles:
            raise_own(0, at, products(before[...], normed_ref[at, :]))

    @pl.when((count_after > low_after) & (own_tail > 0))
    def _():
        for at in tiles:
            raise_own(1, at, products(after[...], normed_ref[at, :]))


def across(chunk, befores, afters, bounds, returned):
    _, _, own_head, own_tail = read_counts(bounds)

    @pl.when((own_head == ROWS) & (own_tail == ROWS))
    def _():
        for i in range(chunk + 1):
            for j in range(chunk + 1):
                if max(i, j) == chunk:
                    across_pieces(befores[i], *TO_AFTER[i], afters[j], *TO_BEFORE[j], bounds, returned)


def across_pieces(before, low_i, size_i, after, low_j, size_j, bounds, returned):
    skip_i = max(0, low_j - low_i)
    size_j = min(size_j, low_i + size_i - low_j)
    if skip_i >= size_i or size_j <= 0:
        return
    low_i, size_i = low_i + skip_i, size_i - skip_i
    rows = before[skip_i : skip_i + size_i, :]
    best = jnp.full((size_i, 128), -1.0, jnp.float32)
    for part in range(0, size_j, TILE):
        size = min(TILE, size_j - part)
        at = pl.ds(low_j + part, size)
        scores = products(rows, after[part : part + size, :])
        bound = bounds[AFTER_BEFORE : AFTER_BEFORE + 1, at]
        masked = jnp.where(places(scores.shape, 0) + low_i >= bound, scores, -1.0)
        raise_peak(returned, 1, at, jnp.max(masked, axis=0, keepdims=True))
        for lanes in range(0, size, 128):
            best = jnp.maximum(best, masked[:, lanes : lanes + 128])
    raise_peak(returned, 0, pl.ds(low_i, size_i), jnp.max(best.T, axis=0, keepdims=True))


def take_chunk(side_0, side_1, before, after):
    for part in range(0, before.shape[0], 128):
        at = slice(part, part + 128)
        before[at, :], after[at, :] = by_role(unit_rows(side_0[at, :]), unit_rows(side_1[at, :]))


def first_kernel(raw_hbm, *refs):
    (first, noted), (normed, ids_ref, _) = (refs[0:2], refs[2:4]), refs[4:7]
    befores, afters = refs[7:10], refs[10:13]
    bounds, peaks, returned = refs[13:16]
    pieces, sems = refs[16:18], refs[18]
    copies = [cut_copy(raw_hbm, 4, side, pieces[side], sems.at[side]) for side in range(2)]
    peaks[...] = jnp.full_like(peaks, -1.0)
    returned[...] = jnp.full_like(returned, -1.0)
    notes = by_role(*(side[2 * EDGE :, :128].astype(jnp.float32) for side in noted))
    find_bounds(ids_ref[...], *notes, bounds)
    got = first, [side.at[pl.ds(0, EDGE)] for side in noted], [side.at[pl.ds(EDGE, EDGE)] for side in noted]
    for chunk in range(3):
        take_chunk(*got[chunk], befores[chunk], afters[chunk])
        against_own(chunk, befores[chunk], afters[chunk], normed, bounds, peaks)
        across(chunk, befores, afters, bounds, returned)
    for copy in copies:
        copy.wait()


def next_kernel(chunk, side_0, side_1, normed, bounds, peaks_in, returned_in, *refs):
    befores, afters = refs[:chunk], refs[chunk : 2 * chunk]
    peaks, returned, before, after = refs[2 * chunk :]
    peaks[...] = peaks_in[...]
    returned[...] = returned_in[...]
    take_chunk(side_0, side_1, before, after)
    against_own(chunk, before, after, normed, bounds, peaks)
    across(chunk, [*befores, before], [*afters, after], bounds, returned)


def last_across_kernel(side_0, side_1, edge_before, edge_after, bounds, returned_in, *refs):
    before, after, returned = refs
    returned[...] = returned_in[...]
    take_chunk(side_0, side_1, before, after)
    across_edges = [None, None, edge_before, None, before], [None, None, edge_after, None, after]
    across(4, *across_edges, bounds, returned)


def last_own_kernel(chunk, before, after, normed, bounds, peaks_in, peaks):
    peaks[...] = peaks_in[...]
    against_own(chunk, before, after, normed, bounds, peaks)


def join_kernel(earlier_in, later_in, peaks, bounds, side_0, side_1, earlier, later):
    from_before, from_after = by_role(side_0[...], side_1[...])
    has_before = bounds[COUNT_BEFORE : COUNT_BEFORE + 1, :] > 0
    has_after = bounds[COUNT_AFTER : COUNT_AFTER + 1, :] > 0
    from_before = jnp.where(has_before, from_before[1:2], -1.0)
    from_after = jnp.where(has_after, from_after[0:1], -1.0)
    earlier[...] = jnp.maximum(jnp.maximum(earlier_in[...], peaks[0:1, :]), from_before)
    later[...] = jnp.maximum(jnp.maximum(later_in[...], peaks[1:2, :]), from_after)


def call(kernel, outs, args, in_hbm=0, scratch=()):
    in_vmem = pl.BlockSpec(memory_space=pltpu.VMEM)
    return pl.pallas_call(
        kernel,
        out_shape=outs,
        in_specs=[pl.BlockSpec(memory_space=pl.ANY)] * in_hbm + [in_vmem] * (len(args) - in_hbm),
        out_specs=[in_vmem] * len(outs),
        scratch_shapes=scratch,
        compiler_params=pltpu.CompilerParams(vmem_limit_bytes=VMEM_LIMIT),
        cost_estimate=pl.CostEstimate(flops=1024, bytes_accessed=1024, transcendentals=0),
    )(*args)


def vectors(count, dtype=jnp.float32):
    return jax.ShapeDtypeStruct((count, ROWS), dtype)


def piece(rows):
    return jax.ShapeDtypeStruct((rows, WIDTH), jnp.bfloat16)


def per_device(embeddings, cluster_ids):
    ids = cluster_ids.reshape(1, ROWS)
    low, size = TO_AFTER[0]
    cut = embeddings[low : low + size]
    first = exchanged(cut, cut)
    cuts = call(
        noted_kernel,
        [piece(2 * EDGE + NOTE)] * 2,
        (embeddings, cut, ids),
        in_hbm=2,
        scratch=[pltpu.SemaphoreType.DMA((4,))],
    )
    noted = exchanged(*cuts)
    (cut,) = call(
        middle_kernel,
        [piece(SIZES[3])],
        (embeddings, *first),
        in_hbm=3,
        scratch=[pltpu.SemaphoreType.DMA],
    )
    middle = exchanged(cut, cut)
    normed, earlier, later = call(
        own_kernel,
        [piece(ROWS), vectors(1), vectors(1)],
        (embeddings, cluster_ids.reshape(ROWS, 1), ids),
    )
    sizes = [piece(size) for size in SIZES]
    *new, bounds, peaks, returned, cut_0, cut_1 = call(
        first_kernel,
        [*sizes[:3], *sizes[:3], vectors(8, jnp.int32), vectors(2), vectors(2), sizes[4], sizes[4]],
        (embeddings, *first, *noted, normed, ids, earlier),
        in_hbm=1,
        scratch=[pltpu.SemaphoreType.DMA((2,))],
    )
    last = exchanged(cut_0, cut_1)
    befores, afters = new[:3], new[3:]
    peaks, returned = call(
        functools.partial(next_kernel, 3),
        [vectors(2), vectors(2)],
        (*middle, normed, bounds, peaks, returned, *befores, *afters),
        scratch=[pltpu.VMEM((SIZES[3], WIDTH), jnp.bfloat16)] * 2,
    )
    before, after, returned = call(
        last_across_kernel,
        [sizes[4], sizes[4], vectors(2)],
        (*last, befores[2], afters[2], bounds, returned),
    )
    sent_back = exchanged(returned, returned)
    (peaks,) = call(
        functools.partial(last_own_kernel, 4),
        [vectors(2)],
        (before, after, normed, bounds, peaks),
    )
    earlier, later = call(
        join_kernel, [vectors(1), vectors(1)], (earlier, later, peaks, bounds, *sent_back)
    )
    return (earlier.reshape(ROWS), later.reshape(ROWS))


def solution(mesh):
    placed = (P(AXES, None), P(AXES))
    return jax.shard_map(
        per_device,
        mesh=mesh,
        in_specs=placed,
        out_specs=(P(AXES), P(AXES)),
        check_vma=False,
    )
```
